256 devices in a mesh: col: 16 (over z, y_lo), chi: 16 (over y_hi, x, core).
Axes of the slice: x: 4, y: 4 (y_hi: 2, y_lo: 2; y = y_hi * 2 + y_lo), z: 8, core: 2. Of those that a mesh axis runs over, the one named last changes fastest.
Arguments:
- left_iso: bfloat16 [16, 256, 20, 256], P('col', 'chi'), may hold values from -0.078125 to 0.078125
- right_iso: bfloat16 [16, 256, 20, 256], P('col', 'chi'), may hold values from -0.078125 to 0.078125
- center: bfloat16 [16, 256, 20, 256], P('col', 'chi'), may hold values from -0.0048828125 to 0.0048828125
- site_tensor: bfloat16 [16, 400, 400], P('col'), may hold values from -0.3125 to 0.3125
- left_env: float32 [16, 256, 20, 256], P('col', 'chi'), may hold values from -6 to 6
- right_env: float32 [16, 256, 20, 256], P('col', 'chi'), may hold values from -6 to 6
Outputs:
- new_left: float32 [16, 256, 20, 256], P('col', 'chi')
- new_right: float32 [16, 256, 20, 256], P('col', 'chi')
- new_center: float32 [16, 256, 20, 256], P('col', 'chi')
The draws below stay inside these ranges and needn't reach their ends.
All inputs are finite; a program needn't handle non-finite values.
Results may differ from the reference program's by a relative error of at most 0.011.
Values may be sent and summed in bfloat16 or wider, within the bound.
A program may use at most 64 MiB of HBM per device.

```python
import jax
import jax.numpy as jnp
from jax import lax

CHI = 256
DD = 20
COLS = 16


def level_of(own_key, extent, shards, smallest, top_value):
    factor_of = 1.0
    for dim, blocks in shards:
        steps = jax.random.uniform(jax.random.fold_in(jax.random.fold_in(own_key, 6), dim), (blocks,), jnp.float32, smallest / len(shards), top_value / len(shards))
        factor_of = factor_of * jnp.repeat(jnp.exp(steps), extent[dim] // blocks).reshape((-1,) + (1,) * (len(extent) - 1 - dim))
    return factor_of


def gaussian(rng, dims, scale, reach, cuts=(), held_as=jnp.bfloat16):
    entries = jax.random.normal(rng, dims, jnp.float32) * scale
    if len(cuts) > 0:
        entries = level_of(rng, dims, cuts, -0.22, 0.18) * entries
    return jnp.clip(entries, min=-reach, max=reach).astype(held_as)


def setup_inputs(seed: int = 0) -> dict:
    key_of = jax.random.split(jax.random.key(seed), 7)
    return {
        "left_iso": gaussian(key_of[0], (COLS, CHI, DD, CHI), (CHI * DD) ** -0.5, 0.078125, ((0, 16), (1, 16))),
        "right_iso": gaussian(key_of[1], (COLS, CHI, DD, CHI), (CHI * DD) ** -0.5, 0.078125, ((0, 16), (1, 16))),
        "center": gaussian(key_of[2], (COLS, CHI, DD, CHI), (CHI * CHI * DD) ** -0.5, 0.0048828125, ((0, 16), (1, 16))),
        "site_tensor": gaussian(key_of[3], (COLS, DD * DD, DD * DD), (DD * DD) ** -0.5, 0.3125, ((0, 16),)),
        "left_env": gaussian(key_of[4], (COLS, CHI, DD, CHI), 1.0, 6.0, ((0, 16), (1, 16)), jnp.float32),
        "right_env": gaussian(key_of[5], (COLS, CHI, DD, CHI), 1.0, 6.0, ((0, 16), (1, 16)), jnp.float32),
    }


def contract(pattern, left_op, right_op):
    return jnp.einsum(pattern, left_op.astype(jnp.float32), right_op.astype(jnp.float32), precision=lax.Precision.HIGHEST)

def left_step(column_args):
    left_env, left_iso, site_tensor = column_args
    bond_width = left_iso.shape[1]
    chi_span = left_iso.shape[0]
    left_b = left_env.astype(jnp.bfloat16)
    section_one = contract('bla,auc->bluc', left_b, left_iso).astype(jnp.bfloat16)
    section_one = section_one.reshape(chi_span, bond_width * bond_width, chi_span)
    section_two = contract('bpc,pq->bqc', section_one, site_tensor).astype(jnp.bfloat16)
    section_two = section_two.reshape(chi_span, bond_width, bond_width, chi_span)
    return contract('bdc,brda->cra', left_iso, section_two)

def right_step(column_args):
    right_env, right_iso, site_tensor = column_args
    bond_width = right_iso.shape[1]
    site_four = site_tensor.reshape(bond_width, bond_width, bond_width, bond_width)
    right_b = right_env.astype(jnp.bfloat16)
    section_one = contract('cre,aue->crua', right_b, right_iso).astype(jnp.bfloat16)
    section_two = contract('crua,lurd->clda', section_one, site_four).astype(jnp.bfloat16)
    return contract('bdc,clda->bla', right_iso, section_two)

def normalize(raw_env):
    total = jnp.sum(raw_env * raw_env)
    return raw_env * jnp.sqrt(raw_env.size / total)

def center_step(column_args):
    left_new, right_new, center, site_tensor = column_args
    bond_width = center.shape[1]
    chi_span = center.shape[0]
    left_nb = left_new.astype(jnp.bfloat16)
    right_nb = right_new.astype(jnp.bfloat16)
    section_one = contract('bla,auc->bluc', left_nb, center).astype(jnp.bfloat16)
    section_one = section_one.reshape(chi_span, bond_width * bond_width, chi_span)
    section_two = contract('bpc,pq->bqc', section_one, site_tensor).astype(jnp.bfloat16)
    section_two = section_two.reshape(chi_span, bond_width, bond_width, chi_span)
    return contract('brda,era->bde', section_two, right_nb)

def reference(left_iso, right_iso, center, site_tensor, left_env, right_env):
    left_raw = lax.map(left_step, (left_env, left_iso, site_tensor))
    right_raw = lax.map(right_step, (right_env, right_iso, site_tensor))
    new_left = jnp.roll(jax.vmap(normalize)(left_raw), 1, axis=0)
    new_right = jnp.roll(jax.vmap(normalize)(right_raw), -1, axis=0)
    new_center = lax.map(center_step, (new_left, new_right, center, site_tensor))
    return (new_left, new_right, new_center)
```

```python
import jax
import jax.numpy as jnp
from jax import lax
from jax.experimental import pallas as pl
from jax.experimental.pallas import tpu as pltpu
from jax.sharding import PartitionSpec as P

MESH = pl.DeviceIdType.MESH
BF = jnp.bfloat16
F32 = jnp.float32
D = 20
DP = 24
CHI = 256
ROWS = 16
HALF = 128
NT = (((1,), (1,)), ((), ()))
NN = (((1,), (0,)), ((), ()))


def dot(a, b, dims=NN):
    return lax.dot_general(a, b, dims, preferred_element_type=F32)


def kernel(
    al_ref, ar_ref, ac_ref, w_ref, l_ref, r_ref,
    new_left_ref, new_right_ref, new_center_ref,
    pad, half_al, half_ar, half_ac, half_r,
    g_al, g_ar, g_ac, g_r, g_n,
    lb, arj, al24, alt, w2, w4, xs, ys, acc, zf, zk,
    sib_s, sib_r, x_s, x_r, raw, lp, lr, ln,
    ry_s, ry_r, rp, rn_r, cy_s, cy_r, sq_s, sq_r,
    send_sem, recv_sem,
):
    col = lax.axis_index("col")
    me = lax.axis_index("chi")
    y, x, c = me // 8, (me // 2) % 4, me % 2
    cols = lax.axis_size("col")

    def at(dcol=0, dy=0, dx=0, dc=0):
        chi = ((y + dy) % 2) * 8 + ((x + dx) % 4) * 2 + (c + dc) % 2
        return ((col + dcol + cols) % cols, chi)

    SIB, YP = at(dc=1), at(dy=1)
    XP = [at(dx=d) for d in (1, 2, 3)]

    barrier = pltpu.get_barrier_semaphore()
    peers = [SIB, YP] + XP + [at(1), at(1, 1), at(-1), at(-1, 1)]
    for p in peers:
        pl.semaphore_signal(barrier, inc=1, device_id=p, device_id_type=MESH)

    count = [0]
    started = []

    def send(src, dst, target):
        i = count[0]
        count[0] += 1
        cp = pltpu.make_async_remote_copy(
            src_ref=src, dst_ref=dst, send_sem=send_sem.at[i], recv_sem=recv_sem.at[i],
            device_id=target, device_id_type=MESH,
        )
        cp.start()
        started.append(cp)
        return cp

    def recv(cps):
        for cp in cps if isinstance(cps, list) else [cps]:
            cp.wait_recv()

    def sent(cp):
        cp.wait_send()
        started[:] = [s for s in started if s is not cp]

    def to_pad(ref):
        for a in range(ROWS):
            v = ref[a].astype(F32)
            pad[0, a * DP:a * DP + D, :] = v[:, :HALF]
            pad[1, a * DP:a * DP + D, :] = v[:, HALF:]

    def padded():
        return jnp.concatenate([pad[0], pad[1]], axis=1)

    def row(h, u):
        return pad[h, pl.ds(u, ROWS, stride=DP), :]

    def halves(g, half):
        for u in range(D):
            for h in range(2):
                half[h, u] = row(h, u).astype(BF)
        g[c, y, x] = half[y]

    def to_x(ref):
        return [send(ref, ref, p) for p in XP]

    def to_y(g, half):
        return send(half.at[1 - y], g.at[c, y, x], YP)

    def own_x(g):
        return to_x(g.at[c, y, x])

    def rest_x(g, first):
        recv(first)
        return to_x(g.at[c, 1 - y, x])

    def to_sib(g, xs_):
        recv(xs_)
        return send(g.at[c], g.at[c], SIB)

    pad[...] = jnp.zeros_like(pad)
    to_pad(al_ref)
    halves(g_al, half_al)
    al24[0] = padded().astype(BF)
    pl.semaphore_wait(barrier, len(peers))
    al_y = to_y(g_al, half_al)
    al_x = own_x(g_al)
    to_pad(r_ref)
    halves(g_r, half_r)
    r_y = to_y(g_r, half_r)
    al_x += rest_x(g_al, al_y)
    r_x = own_x(g_r)
    to_pad(l_ref)
    lb[0] = padded().astype(BF)
    lb_y = send(lb.at[0], lb.at[1], YP)
    al24_y = send(al24.at[0], al24.at[1], YP)
    alt[:, :384] = al24[0].astype(F32).T.astype(BF)
    r_x += rest_x(g_r, r_y)
    to_pad(ar_ref)
    halves(g_ar, half_ar)
    arj[0] = padded().astype(BF)
    ar_y = to_y(g_ar, half_ar)
    arj_y = send(arj.at[0], arj.at[1], YP)
    to_pad(ac_ref)
    halves(g_ac, half_ac)
    ac_y = to_y(g_ac, half_ac)

    def spread(other):
        i = lax.broadcasted_iota(jnp.int32, (D * DP, D * D), 0)
        j = lax.broadcasted_iota(jnp.int32, (D * DP, D * D), 1)
        big = (i * 2731) >> 16
        small = i - big * DP
        want = small * D + big if other else big * D + small
        return jnp.where((small < D) & (j == want), 1.0, 0.0).astype(BF)

    t = dot(spread(True), w_ref[...]).astype(BF)
    w4[...] = dot(t, spread(False), NT).astype(BF)
    w2[...] = w4[...].astype(F32).T.astype(BF)

    def full_rows(g, u):
        return jnp.concatenate(
            [g[cc, yy, xx, u] for yy in range(2) for xx in range(4) for cc in range(2)], axis=0
        )

    def pair_half(g, u2):
        return jnp.concatenate([full_rows(g, 2 * u2), full_rows(g, 2 * u2 + 1)], axis=1)

    def step_one(lhs_ref, g):
        def body(u2, _):
            rhs = pair_half(g, u2)
            for k in range(2):
                out = dot(lhs_ref[k], rhs)
                xs[u2, 16 * k:16 * k + 16] = out.reshape(16, DP, CHI)
            return 0
        lax.fori_loop(0, D // 2, body, 0)

    def step_two(m_ref):
        def body(p, _):
            rows = []
            for u2 in range(D // 2):
                v0, v1 = xs[u2, 2 * p], xs[u2, 2 * p + 1]
                rows.append(jnp.concatenate([v0[:, :HALF], v1[:, :HALF]], axis=1))
                rows.append(jnp.concatenate([v0[:, HALF:], v1[:, HALF:]], axis=1))
            rhs = jnp.concatenate(rows, axis=0).astype(BF)
            out = dot(m_ref[...], rhs)
            for r2 in range(D // 2):
                o0 = out[2 * r2 * DP:(2 * r2 + 1) * DP]
                o1 = out[(2 * r2 + 1) * DP:(2 * r2 + 2) * DP]
                top = jnp.concatenate([o0[:, :HALF], o1[:, :HALF]], axis=1)
                low = jnp.concatenate([o0[:, HALF:], o1[:, HALF:]], axis=1)
                ys[r2, p] = jnp.concatenate([top, low], axis=0).astype(BF)
            return 0
        lax.fori_loop(0, 16, body, 0)

    def step_three(g):
        acc[...] = jnp.zeros_like(acc)

        def body(n2, _):
            rhs = pair_half(g, n2)
            for k in range(2):
                lhs = ys[n2, 8 * k:8 * k + 8].reshape(384, CHI)
                acc[k] += dot(lhs, rhs, NT)
            return 0
        lax.fori_loop(0, D // 2, body, 0)

    def sum_all(part, slot):
        sq_s[slot, 0] = part
        cp = send(sq_s.at[slot, 0], sq_r.at[slot, 0], SIB)
        recv(cp)
        part = part + sq_r[slot, 0]
        sq_s[slot, 1] = part
        cp = send(sq_s.at[slot, 1], sq_r.at[slot, 1], YP)
        recv(cp)
        part = part + sq_r[slot, 1]
        sq_s[slot, 2] = part
        cps = [send(sq_s.at[slot, 2], sq_r.at[slot, 2 + d], XP[d]) for d in range(3)]
        recv(cps)
        part = part + sq_r[slot, 2] + sq_r[slot, 3] + sq_r[slot, 4]
        total = jnp.sum(part)
        return jnp.sqrt(float(CHI * D * CHI) / total)

    al_sib = to_sib(g_al, al_x)
    ar_x = own_x(g_ar) + rest_x(g_ar, ar_y)
    recv([al24_y, lb_y, al_sib])
    alt[:, 384:] = al24[1].astype(F32).T.astype(BF)
    step_one(lb, g_al)
    step_two(w2)
    sib = []
    for ch in range(2):
        def body(k, _):
            r2 = ch * 5 + k
            zf[...] = dot(alt[...], ys[r2].reshape(768, CHI)).reshape(8, 2, ROWS, CHI)
            sib_s[r2] = zf[:, 1 - c].astype(BF)
            zk[r2] = zf[:, c]
            return 0
        lax.fori_loop(0, 5, body, 0)
        part_of = pl.ds(ch * 5, 5)
        sib.append(send(sib_s.at[part_of], sib_r.at[part_of], SIB))
    rs = []
    for ch in range(2):
        recv(sib[ch])
        for k in range(5):
            r2 = ch * 5 + k
            v = zk[r2] + sib_r[r2].astype(F32)
            zk[r2] = v
            for yy in range(2):
                for xx in range(4):
                    x_s[xx, r2, yy] = v[yy * 4 + xx].astype(BF)
        part_of = pl.ds(ch * 5, 5)
        for d in (1, 2, 3):
            to = (x + d) % 4
            rs.append(send(x_s.at[to, part_of], x_r.at[d - 1, part_of], XP[d - 1]))
    r_sib = to_sib(g_r, r_x)
    ac_x = own_x(g_ac) + rest_x(g_ac, ac_y)
    recv([arj_y, r_sib])
    step_one(arj, g_r)
    recv(rs)
    part = jnp.zeros((8, HALF), F32)
    for r2 in range(D // 2):
        for yy in range(2):
            v = zk[r2, yy * 4 + x]
            for d in range(3):
                v = v + x_r[d, r2, yy].astype(F32)
            raw[r2, yy] = v
            s = v * v
            s = s[:, :HALF] + s[:, HALF:]
            part = part + s[:8] + s[8:]
    scale = sum_all(part, 1)
    lp[...] = (raw[...] * scale).astype(BF)
    l_col = [send(lp, lr.at[y], at(1)), send(lp, lr.at[y], at(1, 1))]

    step_two(w4)
    ar_sib = to_sib(g_ar, ar_x)
    recv(ar_sib)
    step_three(g_ar)
    ry_s[...] = acc[1].astype(BF)
    ry = send(ry_s, ry_r, YP)
    ac_sib = to_sib(g_ac, ac_x)
    recv(ry)
    right = acc[0] + ry_r[...].astype(F32)
    pad[0] = right[:, :HALF]
    pad[1] = right[:, HALF:]
    sqr = right * right
    part = jnp.sum((sqr[:, :HALF] + sqr[:, HALF:]).reshape(48, 8, HALF), axis=0)
    scale = sum_all(part, 0)
    for h in range(2):
        for u in range(D):
            rp[h, u] = (row(h, u) * scale).astype(BF)
    n_own = send(rp.at[y], g_n.at[c, y, x], at(-1))
    n_other = send(rp.at[1 - y], g_n.at[c, y, x], at(-1, 1))
    n_rest = send(rp.at[1 - y], rn_r, at(-1))

    recv(l_col)
    sent(lb_y)
    ln[...] = jnp.zeros_like(ln)
    for yy in range(2):
        for src in range(2):
            for l in range(D):
                h = l % 2
                v = lr[src, l // 2, yy, :, h * HALF:(h + 1) * HALF].astype(F32)
                ln[yy, src, pl.ds(l, ROWS, stride=DP), :] = v
    for yy in range(2):
        lb[yy] = jnp.concatenate([ln[yy, 0], ln[yy, 1]], axis=1).astype(BF)
    recv(ac_sib)
    step_one(lb, g_ac)
    recv([n_own, n_other])
    n_x = own_x(g_n) + to_x(g_n.at[c, 1 - y, x])
    step_two(w2)
    n_sib = to_sib(g_n, n_x)
    lnew = jnp.concatenate([ln[y, 0], ln[y, 1]], axis=1)
    new_left_ref[...] = lnew.reshape(ROWS, DP, CHI)[:, :D]
    recv(n_rest)
    for l in range(D):
        pad[y, pl.ds(l, ROWS, stride=DP), :] = g_n[c, y, x, l].astype(F32)
        pad[1 - y, pl.ds(l, ROWS, stride=DP), :] = rn_r[l].astype(F32)
    new_right_ref[...] = padded().reshape(ROWS, DP, CHI)[:, :D]
    recv(n_sib)
    step_three(g_n)
    cy_s[...] = acc[1 - y].astype(BF)
    cy = send(cy_s, cy_r, YP)
    recv(cy)
    center = acc[y] + cy_r[...].astype(F32)
    new_center_ref[...] = center.reshape(ROWS, DP, CHI)[:, :D]
    for cp in started:
        cp.wait_send()


def on_device(left_iso, right_iso, center, site_tensor, left_env, right_env):
    out = jax.ShapeDtypeStruct((ROWS, D, CHI), F32)
    vm = pl.BlockSpec(memory_space=pltpu.VMEM)
    V = pltpu.VMEM
    res = pl.pallas_call(
        kernel,
        out_shape=[out] * 3,
        in_specs=[vm] * 6,
        out_specs=[vm] * 3,
        scratch_shapes=[
            V((2, ROWS * DP, HALF), F32),
            *[V((2, D, ROWS, HALF), BF)] * 4,
            *[V((2, 2, 4, D, ROWS, HALF), BF)] * 5,
            *[V((2, ROWS * DP, CHI), BF)] * 3,
            V((CHI, 2 * ROWS * DP), BF),
            V((D * DP, D * DP), BF), V((D * DP, D * DP), BF),
            V((D // 2, 32, DP, CHI), F32),
            V((D // 2, 16, 2 * DP, CHI), BF),
            V((2, ROWS * DP, CHI), F32),
            V((8, 2, ROWS, CHI), F32),
            V((D // 2, 8, ROWS, CHI), F32),
            V((D // 2, 8, ROWS, CHI), BF), V((D // 2, 8, ROWS, CHI), BF),
            V((4, D // 2, 2, ROWS, CHI), BF), V((3, D // 2, 2, ROWS, CHI), BF),
            V((D // 2, 2, ROWS, CHI), F32),
            V((D // 2, 2, ROWS, CHI), BF), V((2, D // 2, 2, ROWS, CHI), BF),
            V((2, 2, ROWS * DP, HALF), F32),
            V((ROWS * DP, CHI), BF), V((ROWS * DP, CHI), BF),
            V((2, D, ROWS, HALF), BF), V((D, ROWS, HALF), BF),
            V((ROWS * DP, CHI), BF), V((ROWS * DP, CHI), BF),
            V((2, 3, 8, HALF), F32), V((2, 5, 8, HALF), F32),
            pltpu.SemaphoreType.DMA((72,)), pltpu.SemaphoreType.DMA((72,)),
        ],
        compiler_params=pltpu.CompilerParams(
            collective_id=0, has_side_effects=True, vmem_limit_bytes=56 * 2**20
        ),
        cost_estimate=pl.CostEstimate(flops=9 * 10**9, bytes_accessed=3 * 10**6, transcendentals=0),
        name="vumps",
    )(left_iso[0], right_iso[0], center[0], site_tensor[0], left_env[0], right_env[0])
    return tuple(o[None] for o in res)


def solution(mesh):
    spec = P("col", "chi", None, None)
    return jax.shard_map(
        on_device,
        mesh=mesh,
        in_specs=(spec, spec, spec, P("col", None, None), spec, spec),
        out_specs=(spec, spec, spec),
        check_vma=False,
    )
```

```python
import jax
import jax.numpy as jnp
from jax import lax
from jax.experimental import pallas as pl
from jax.experimental.pallas import tpu as pltpu
from jax.sharding import PartitionSpec as P

MESH = pl.DeviceIdType.MESH
BF = jnp.bfloat16
F32 = jnp.float32
D = 20
DP = 24
CHI = 256
ROWS = 16
HALF = 128
NT = (((1,), (1,)), ((), ()))
NN = (((1,), (0,)), ((), ()))


def dot(a, b, dims=NN):
    return lax.dot_general(a, b, dims, preferred_element_type=F32)


def kernel(
    al_ref, ar_ref, ac_ref, w_ref, l_ref, r_ref,
    new_left_ref, new_right_ref, new_center_ref,
    pad, half_r, p_al, p_ar, lbf, lbp,
    g_al, g_ar, g_ac, g_r, g_n,
    lb, arj, alt, w2, w4, xs, ys, acc, zf, zk,
    sib_s, sib_r, x_s, x_r, raw, lp, lr, ln,
    rs_s, n_in, n_sum, n_snd, n_oth, cy_s, cy_r, sq_s, sq_r, sc_s, sc_r,
    send_sem, recv_sem,
):
    col = lax.axis_index("col")
    me = lax.axis_index("chi")
    y, x, c = me // 8, (me // 2) % 4, me % 2
    cols = lax.axis_size("col")

    def at(dcol=0, dy=0, dx=0, dc=0):
        chi = ((y + dy) % 2) * 8 + ((x + dx) % 4) * 2 + (c + dc) % 2
        return ((col + dcol + cols) % cols, chi)

    SIB, YP = at(dc=1), at(dy=1)
    XP = [at(dx=d) for d in (1, 2, 3)]

    barrier = pltpu.get_barrier_semaphore()
    peers = [SIB, YP] + XP + [at(1), at(1, 1), at(-1), at(-1, 1)]
    for p in peers:
        pl.semaphore_signal(barrier, inc=1, device_id=p, device_id_type=MESH)

    count = [0]
    started = []

    def send(src, dst, target):
        i = count[0]
        count[0] += 1
        cp = pltpu.make_async_remote_copy(
            src_ref=src, dst_ref=dst, send_sem=send_sem.at[i], recv_sem=recv_sem.at[i],
            device_id=target, device_id_type=MESH,
        )
        cp.start()
        started.append(cp)
        return cp

    def recv(cps):
        for cp in cps if isinstance(cps, list) else [cps]:
            cp.wait_recv()

    def own_half(v):
        return jnp.where(y == 0, v[..., :HALF], v[..., HALF:])

    def other_half(v):
        return jnp.where(y == 0, v[..., HALF:], v[..., :HALF])

    def lanes(ref, h):
        return ref.at[:, :, pl.ds(pl.multiple_of(h * HALF, HALF), HALF)]

    def put(h, u, v):
        pad[h, pl.ds(u, ROWS, stride=DP), :] = v.astype(F32)

    def row(h, u):
        return pad[h, pl.ds(u, ROWS, stride=DP), :]

    def padded():
        return jnp.concatenate([pad[0], pad[1]], axis=1)

    def pad_own(ref):
        for u in range(D):
            v = ref[u].astype(F32)
            put(0, u, v[:, :HALF])
            put(1, u, v[:, HALF:])
        return padded()

    def pad_partner(g, p):
        for u in range(D):
            put(y, u, g[c, x, 1 - y, u])
            put(1 - y, u, p[u])
        return padded()

    def to_x(ref):
        return [send(ref, ref, p) for p in XP]

    def to_y(g, src):
        return send(src, g.at[c, x, y], YP)

    def own_x(g):
        return to_x(g.at[c, x, y])

    def rest_x(g, first):
        recv(first)
        return to_x(g.at[c, x, 1 - y])

    def to_sib(g, xs_):
        recv(xs_)
        return send(g.at[c], g.at[c], SIB)

    g_al[c, x, y] = own_half(al_ref[...])
    half_r[...] = other_half(r_ref[...]).astype(BF)
    g_r[c, x, y] = own_half(r_ref[...]).astype(BF)
    pad[...] = jnp.zeros_like(pad)
    pl.semaphore_wait(barrier, len(peers))
    al_y = to_y(g_al, lanes(al_ref, 1 - y))
    al_x = own_x(g_al)
    r_y = to_y(g_r, half_r)
    lbf[...] = l_ref[...].astype(BF)
    lb_y = send(lbf, lbp, YP)
    p_al_y = send(lanes(al_ref, y), p_al, YP)
    ar_y = to_y(g_ar, lanes(ar_ref, 1 - y))
    p_ar_y = send(lanes(ar_ref, y), p_ar, YP)
    ac_y = to_y(g_ac, lanes(ac_ref, 1 - y))
    g_ar[c, x, y] = own_half(ar_ref[...])
    g_ac[c, x, y] = own_half(ac_ref[...])
    al_x += rest_x(g_al, al_y)
    r_x = own_x(g_r) + rest_x(g_r, r_y)
    ar_x = own_x(g_ar)
    lb[0] = pad_own(l_ref).astype(BF)
    alt[:, :384] = pad_own(al_ref).T.astype(BF)
    arj[0] = pad_own(ar_ref).astype(BF)
    ln[...] = jnp.zeros_like(ln)

    def spread(other):
        i = lax.broadcasted_iota(jnp.int32, (D * DP, D * D), 0)
        j = lax.broadcasted_iota(jnp.int32, (D * DP, D * D), 1)
        big = (i * 2731) >> 16
        small = i - big * DP
        want = small * D + big if other else big * D + small
        return jnp.where((small < D) & (j == want), 1.0, 0.0).astype(BF)

    t = dot(spread(True), w_ref[...]).astype(BF)
    w4[...] = dot(t, spread(False), NT).astype(BF)
    w2[...] = w4[...].astype(F32).T.astype(BF)

    def full_rows(g, u):
        return jnp.concatenate(
            [g[cc, xx, yy, u] for yy in range(2) for xx in range(4) for cc in range(2)], axis=0
        )

    def pair_half(g, u2):
        return jnp.concatenate([full_rows(g, 2 * u2), full_rows(g, 2 * u2 + 1)], axis=1)

    def run(n, body, hooks=()):
        begin = 0
        for i, f in list(hooks) + [(n, None)]:
            lax.fori_loop(begin, i, lambda k, _: body(k), None)
            begin = i
            if f is not None:
                f()

    def step_one(lhs_ref, g, hooks=()):
        def body(q):
            rhs = jnp.concatenate([pair_half(g, 5 * q + i) for i in range(5)], axis=1)
            for k in range(2):
                out = dot(lhs_ref[k], rhs)
                for i in range(5):
                    xs[5 * q + i, 16 * k:16 * k + 16] = out[:, i * CHI:(i + 1) * CHI].reshape(16, DP, CHI)
        run(D // 2 // 5, body, hooks)

    def step_two(m_ref, hooks=()):
        def body(q):
            cols_ = []
            for i in range(4):
                p = 4 * q + i
                rows = []
                for u2 in range(D // 2):
                    v0, v1 = xs[u2, 2 * p], xs[u2, 2 * p + 1]
                    rows.append(jnp.concatenate([v0[:, :HALF], v1[:, :HALF]], axis=1))
                    rows.append(jnp.concatenate([v0[:, HALF:], v1[:, HALF:]], axis=1))
                cols_.append(jnp.concatenate(rows, axis=0).astype(BF))
            both = dot(m_ref[...], jnp.concatenate(cols_, axis=1))
            for i in range(4):
                out = both[:, i * CHI:(i + 1) * CHI]
                for r2 in range(D // 2):
                    o0 = out[2 * r2 * DP:(2 * r2 + 1) * DP]
                    o1 = out[(2 * r2 + 1) * DP:(2 * r2 + 2) * DP]
                    top = jnp.concatenate([o0[:, :HALF], o1[:, :HALF]], axis=1)
                    low = jnp.concatenate([o0[:, HALF:], o1[:, HALF:]], axis=1)
                    ys[r2, 4 * q + i] = jnp.concatenate([top, low], axis=0).astype(BF)
        run(16 // 4, body, hooks)

    def step_three(g, k):
        def body(n2):
            lhs = jnp.concatenate([ys[i, pl.ds(8 * k, 8)].reshape(384, CHI) for i in range(10)], axis=1)
            rhs = jnp.concatenate([pair_half(g, i) for i in range(10)], axis=1)
            acc[k] = dot(lhs, rhs, NT)
        body(0)
        pad[0] = acc[k, :, :HALF]
        pad[1] = acc[k, :, HALF:]

    def sum_all(part, slot):
        sq_s[slot, 0] = part
        cp = send(sq_s.at[slot, 0], sq_r.at[slot, 0], SIB)
        recv(cp)
        part = part + sq_r[slot, 0]
        sq_s[slot, 1] = part
        cp = send(sq_s.at[slot, 1], sq_r.at[slot, 1], YP)
        recv(cp)
        part = part + sq_r[slot, 1]
        sq_s[slot, 2] = part
        cps = [send(sq_s.at[slot, 2], sq_r.at[slot, 2 + d], XP[d]) for d in range(3)]
        recv(cps)
        part = part + sq_r[slot, 2] + sq_r[slot, 3] + sq_r[slot, 4]
        total = jnp.sum(part)
        return jnp.sqrt(float(CHI * D * CHI) / total)

    def squares(v):
        s = v * v
        if s.shape[1] > HALF:
            s = s[:, :HALF] + s[:, HALF:]
        return s[:8] + s[8:]

    al_sib = to_sib(g_al, al_x)
    ar_x += rest_x(g_ar, ar_y)
    recv([p_al_y, lb_y])
    alt[:, 384:] = pad_partner(g_al, p_al).T.astype(BF)
    lb[1] = pad_own(lbp).astype(BF)
    recv(al_sib)
    step_one(lb, g_al)
    step_two(w2)
    r_sib = to_sib(g_r, r_x)
    recv(p_ar_y)
    arj[1] = pad_partner(g_ar, p_ar).astype(BF)
    sib = []
    for ch in range(2):
        def z_body(k):
            rhs = jnp.concatenate([ys[ch * 5 + 5 * k + i].reshape(768, CHI) for i in range(5)], axis=1)
            out = dot(alt[...], rhs)
            for i in range(5):
                r2 = ch * 5 + 5 * k + i
                zf[...] = out[:, i * CHI:(i + 1) * CHI].reshape(8, 2, ROWS, CHI)
                sib_s[r2] = zf[:, 1 - c].astype(BF)
                zk[r2] = zf[:, c]
        run(5 // 5, z_body)
        part_of = pl.ds(ch * 5, 5)
        sib.append(send(sib_s.at[part_of], sib_r.at[part_of], SIB))
    rs = []
    for ch in range(2):
        recv(sib[ch])
        for k in range(5):
            r2 = ch * 5 + k
            v = zk[r2] + sib_r[r2].astype(F32)
            zk[r2] = v
            for yy in range(2):
                for xx in range(4):
                    x_s[xx, r2, yy] = v[yy * 4 + xx].astype(BF)
        part_of = pl.ds(ch * 5, 5)
        for d in (1, 2, 3):
            to = (x + d) % 4
            rs.append(send(x_s.at[to, part_of], x_r.at[d - 1, part_of], XP[d - 1]))
    ac_x = own_x(g_ac) + rest_x(g_ac, ac_y)

    recv(r_sib)
    step_one(arj, g_r)
    step_two(w4, [(2, lambda: None)])
    recv(rs)
    part = jnp.zeros((8, HALF), F32)
    for r2 in range(D // 2):
        for yy in range(2):
            v = zk[r2, yy * 4 + x]
            for d in range(3):
                v = v + x_r[d, r2, yy].astype(F32)
            lp[r2, yy] = v.astype(BF)
            part = part + squares(v)
    l_col = [send(lp, lr.at[y], at(1)), send(lp, lr.at[y], at(1, 1))]
    left_part = part
    ar_sib = to_sib(g_ar, ar_x)
    scale = sum_all(left_part, 1)
    sc_s[...] = jnp.full((8, HALF), 1.0, F32) * scale
    l_sc = send(sc_s, sc_r, at(1))
    recv(ar_sib)
    n_col = []
    for k, blk in ((0, y), (1, 1 - y)):
        step_three(g_ar, k)
        for h in range(2):
            for l in range(D):
                rs_s[h, k, l] = row(h, l).astype(BF)
        n_col.append(send(rs_s.at[y, k], n_in.at[y, blk], at(-1)))
        n_col.append(send(rs_s.at[1 - y, k], n_in.at[y, blk], at(-1, 1)))

    ac_sib = to_sib(g_ac, ac_x)
    recv(l_col + [l_sc])
    scale = sc_r[0:1, 0:1]
    for l in range(D):
        h = l % 2
        for src in range(2):
            for yy in range(2):
                v = lr[src, l // 2, yy, :, h * HALF:(h + 1) * HALF].astype(F32) * scale
                ln[yy, src, pl.ds(l, ROWS, stride=DP), :] = v
    for yy in range(2):
        lb[yy] = jnp.concatenate([ln[yy, 0], ln[yy, 1]], axis=1).astype(BF)
    for l in range(D):
        for src in range(2):
            new_left_ref[l, :, src * HALF:(src + 1) * HALF] = ln[y, src, pl.ds(l, ROWS, stride=DP), :]
    recv(ac_sib)
    step_one(lb, g_ac)
    recv(n_col)
    part = jnp.zeros((8, HALF), F32)
    for yy in range(2):
        for l in range(D):
            v = n_in[0, yy, l].astype(F32) + n_in[1, yy, l].astype(F32)
            n_sum[yy, l] = v
            g_n[c, x, yy, l] = v.astype(BF)
            part = part + squares(v)
    n_x = to_x(g_n.at[c, x])
    n_snd[...] = n_sum[1 - y].astype(BF)
    n_y = send(n_snd, n_oth, YP)
    step_two(w2)
    n_sib = to_sib(g_n, n_x)
    scale = sum_all(part, 0)
    recv(n_y)
    for l in range(D):
        a, b = n_sum[y, l] * scale, n_oth[l].astype(F32) * scale
        new_right_ref[l, :, :HALF] = jnp.where(y == 0, a, b)
        new_right_ref[l, :, HALF:] = jnp.where(y == 0, b, a)
    recv(n_sib)
    step_three(g_n, 1 - y)
    cy_s[...] = acc[1 - y].astype(BF)
    cy = send(cy_s, cy_r, YP)
    step_three(g_n, y)
    recv(cy)
    pad[0] = (acc[y, :, :HALF] + cy_r[:, :HALF].astype(F32)) * scale
    pad[1] = (acc[y, :, HALF:] + cy_r[:, HALF:].astype(F32)) * scale
    for n in range(D):
        new_center_ref[n, :, :HALF] = row(0, n)
        new_center_ref[n, :, HALF:] = row(1, n)
    for cp in started:
        cp.wait_send()


def on_device(left_iso, right_iso, center, site_tensor, left_env, right_env):
    out = jax.ShapeDtypeStruct((D, ROWS, CHI), F32)
    vm = pl.BlockSpec(memory_space=pltpu.VMEM)
    V = pltpu.VMEM
    res = pl.pallas_call(
        kernel,
        out_shape=[out] * 3,
        in_specs=[vm] * 6,
        out_specs=[vm] * 3,
        scratch_shapes=[
            V((2, ROWS * DP, HALF), F32),
            *[V((D, ROWS, HALF), BF)] * 3,
            *[V((D, ROWS, CHI), BF)] * 2,
            *[V((2, 4, 2, D, ROWS, HALF), BF)] * 5,
            *[V((2, ROWS * DP, CHI), BF)] * 2,
            V((CHI, 2 * ROWS * DP), BF),
            V((D * DP, D * DP), BF), V((D * DP, D * DP), BF),
            V((D // 2, 32, DP, CHI), F32),
            V((D // 2, 16, 2 * DP, CHI), BF),
            V((2, ROWS * DP, CHI), F32),
            V((8, 2, ROWS, CHI), F32),
            V((D // 2, 8, ROWS, CHI), F32),
            V((D // 2, 8, ROWS, CHI), BF), V((D // 2, 8, ROWS, CHI), BF),
            V((4, D // 2, 2, ROWS, CHI), BF), V((3, D // 2, 2, ROWS, CHI), BF),
            V((8, HALF), F32),
            V((D // 2, 2, ROWS, CHI), BF), V((2, D // 2, 2, ROWS, CHI), BF),
            V((2, 2, ROWS * DP, HALF), F32),
            V((2, 2, D, ROWS, HALF), BF), V((2, 2, D, ROWS, HALF), BF),
            V((2, D, ROWS, HALF), F32),
            V((D, ROWS, HALF), BF), V((D, ROWS, HALF), BF),
            V((ROWS * DP, CHI), BF), V((ROWS * DP, CHI), BF),
            V((2, 3, 8, HALF), F32), V((2, 5, 8, HALF), F32),
            V((8, HALF), F32), V((8, HALF), F32),
            pltpu.SemaphoreType.DMA((72,)), pltpu.SemaphoreType.DMA((72,)),
        ],
        compiler_params=pltpu.CompilerParams(
            collective_id=0, has_side_effects=True, vmem_limit_bytes=56 * 2**20
        ),
        cost_estimate=pl.CostEstimate(flops=9 * 10**9, bytes_accessed=3 * 10**6, transcendentals=0),
        name="vumps",
    )(
        *(v[0].transpose(1, 0, 2) for v in (left_iso, right_iso, center)),
        site_tensor[0],
        *(v[0].transpose(1, 0, 2) for v in (left_env, right_env)),
    )
    return tuple(o.transpose(1, 0, 2)[None] for o in res)


def solution(mesh):
    spec = P("col", "chi", None, None)
    return jax.shard_map(
        on_device,
        mesh=mesh,
        in_specs=(spec, spec, spec, P("col", None, None), spec, spec),
        out_specs=(spec, spec, spec),
        check_vma=False,
    )
```

```python
import jax
import jax.numpy as jnp
from jax import lax
from jax.experimental import pallas as pl
from jax.experimental.pallas import tpu as pltpu
from jax.sharding import PartitionSpec as P

MESH = pl.DeviceIdType.MESH
BF = jnp.bfloat16
F32 = jnp.float32
D = 20
DP = 24
CHI = 256
ROWS = 16
HALF = 128
NT = (((1,), (1,)), ((), ()))
NN = (((1,), (0,)), ((), ()))


def dot(a, b, dims=NN):
    return lax.dot_general(a, b, dims, preferred_element_type=F32)


def kernel(
    al_ref, ar_ref, ac_ref, w_ref, l_ref, r_ref,
    new_left_ref, new_right_ref, new_center_ref,
    pad, half_r, p_al, p_ar, lbf, lbp,
    g_al, g_ar, g_ac, g_r, g_n,
    lb, arj, alt, w2, w4, xs, ys, ys2, acc, zf, zk,
    sib_s, sib_r, x_s, x_r, raw, lp, lr, ln,
    rs_s, n_in, n_sum, n_snd, n_oth, cy_s, cy_r, sq_s, sq_r,
    send_sem, recv_sem,
):
    col = lax.axis_index("col")
    me = lax.axis_index("chi")
    y, x, c = me // 8, (me // 2) % 4, me % 2
    cols = lax.axis_size("col")

    def at(dcol=0, dy=0, dx=0, dc=0):
        chi = ((y + dy) % 2) * 8 + ((x + dx) % 4) * 2 + (c + dc) % 2
        return ((col + dcol + cols) % cols, chi)

    SIB, YP = at(dc=1), at(dy=1)
    XP = [at(dx=d) for d in (1, 2, 3)]

    barrier = pltpu.get_barrier_semaphore()
    SY = at(dy=1, dc=1)
    peers = [SIB, YP, SY] + XP + [at(d, 0, k) for d in (1, -1) for k in range(4)] + [at(1, 1), at(-1, 1)]
    for p in peers:
        pl.semaphore_signal(barrier, inc=1, device_id=p, device_id_type=MESH)

    count = [0]
    started = []

    def send(src, dst, target):
        i = count[0]
        count[0] += 1
        cp = pltpu.make_async_remote_copy(
            src_ref=src, dst_ref=dst, send_sem=send_sem.at[i], recv_sem=recv_sem.at[i],
            device_id=target, device_id_type=MESH,
        )
        cp.start()
        started.append(cp)
        return cp

    def recv(cps):
        for cp in cps if isinstance(cps, list) else [cps]:
            cp.wait_recv()

    def own_half(v):
        return jnp.where(y == 0, v[..., :HALF], v[..., HALF:])

    def other_half(v):
        return jnp.where(y == 0, v[..., HALF:], v[..., :HALF])

    def lanes(ref, h):
        return ref.at[:, :, pl.ds(pl.multiple_of(h * HALF, HALF), HALF)]

    def put(h, u, v):
        pad[h, pl.ds(u, ROWS, stride=DP), :] = v.astype(F32)

    def row(h, u):
        return pad[h, pl.ds(u, ROWS, stride=DP), :]

    def padded():
        return jnp.concatenate([pad[0], pad[1]], axis=1)

    def pad_own(ref):
        for u in range(D):
            v = ref[u].astype(F32)
            put(0, u, v[:, :HALF])
            put(1, u, v[:, HALF:])
        return padded()

    def pad_partner(g, p):
        for u in range(D):
            put(y, u, g[c, x, 1 - y, u])
            put(1 - y, u, p[u])
        return padded()

    def to_y(g, src):
        return send(src, g.at[c, x, y], YP)

    def both_ways(g, yy):
        ref = g.at[c, x, yy]
        return send(ref, ref, XP[0]), send(ref, ref, XP[2])

    def own_x(g):
        return list(both_ways(g, y))

    def rest_x(ring, g, first):
        recv(first)
        ring.extend(both_ways(g, 1 - y))

    def hand_up(ring, g):
        recv(ring[0])
        ref = g.at[c, (x + 3) % 4, y]
        ring.append(send(ref, ref, XP[0]))

    def hand_down(ring, g):
        recv(ring[3])
        ref = g.at[c, (x + 1) % 4, 1 - y]
        ring.append(send(ref, ref, XP[2]))

    def to_sib(g, ring):
        recv([ring[1], ring[2], ring[4], ring[5]])
        return send(g.at[c], g.at[c], SIB)

    def straight(ref):
        return [send(ref, ref, p) for p in XP]

    def straight_both(g, first):
        cps = straight(g.at[c, x, y])
        recv(first)
        return cps + straight(g.at[c, x, 1 - y])

    def all_to_sib(g, cps):
        recv(cps)
        return send(g.at[c], g.at[c], SIB)

    g_al[c, x, y] = own_half(al_ref[...])
    half_r[...] = other_half(r_ref[...]).astype(BF)
    g_r[c, x, y] = own_half(r_ref[...]).astype(BF)
    pad[...] = jnp.zeros_like(pad)
    pl.semaphore_wait(barrier, len(peers))
    al_y = to_y(g_al, lanes(al_ref, 1 - y))
    al_x = own_x(g_al)
    r_y = to_y(g_r, half_r)
    lbf[...] = l_ref[...].astype(BF)
    lb_y = send(lbf, lbp, YP)
    p_al_y = send(lanes(al_ref, y), p_al, YP)
    ar_y = to_y(g_ar, lanes(ar_ref, 1 - y))
    p_ar_y = send(lanes(ar_ref, y), p_ar, YP)
    ac_y = to_y(g_ac, lanes(ac_ref, 1 - y))
    rest_x(al_x, g_al, al_y)
    hand_up(al_x, g_al)
    r_x = own_x(g_r)
    g_ar[c, x, y] = own_half(ar_ref[...])
    g_ac[c, x, y] = own_half(ac_ref[...])
    lb[0] = pad_own(l_ref).astype(BF)
    alt[:, :384] = pad_own(al_ref).T.astype(BF)
    hand_down(al_x, g_al)
    rest_x(r_x, g_r, r_y)
    arj[0] = pad_own(ar_ref).astype(BF)
    ln[...] = jnp.zeros_like(ln)

    def spread(other):
        i = lax.broadcasted_iota(jnp.int32, (D * DP, D * D), 0)
        j = lax.broadcasted_iota(jnp.int32, (D * DP, D * D), 1)
        big = (i * 2731) >> 16
        small = i - big * DP
        want = small * D + big if other else big * D + small
        return jnp.where((small < D) & (j == want), 1.0, 0.0).astype(BF)

    t = dot(spread(True), w_ref[...]).astype(BF)
    w4[...] = dot(t, spread(False), NT).astype(BF)
    w2[...] = w4[...].astype(F32).T.astype(BF)

    def full_rows(g, u):
        return jnp.concatenate(
            [g[cc, xx, yy, u] for yy in range(2) for xx in range(4) for cc in range(2)], axis=0
        )

    def pair_half(g, u2):
        return jnp.concatenate([full_rows(g, 2 * u2), full_rows(g, 2 * u2 + 1)], axis=1)

    def run(n, body):
        lax.fori_loop(0, n, lambda k, _: body(k), None)

    def step_one(lhs_ref, g):
        def body(q):
            rhs = jnp.concatenate([pair_half(g, 5 * q + i) for i in range(5)], axis=1)
            for k in range(2):
                out = dot(lhs_ref[k], rhs)
                for i in range(5):
                    xs[5 * q + i, 16 * k:16 * k + 16] = out[:, i * CHI:(i + 1) * CHI].reshape(16, DP, CHI)
        run(D // 2 // 5, body)

    def step_two(m_ref, ys, scale=None):
        def body(q):
            cols_ = []
            for i in range(4):
                p = 4 * q + i
                rows = []
                for u2 in range(D // 2):
                    v0, v1 = xs[u2, 2 * p], xs[u2, 2 * p + 1]
                    rows.append(jnp.concatenate([v0[:, :HALF], v1[:, :HALF]], axis=1))
                    rows.append(jnp.concatenate([v0[:, HALF:], v1[:, HALF:]], axis=1))
                cols_.append(jnp.concatenate(rows, axis=0).astype(BF))
            both = dot(m_ref[...], jnp.concatenate(cols_, axis=1))
            if scale is not None:
                both = both * scale
            for i in range(4):
                out = both[:, i * CHI:(i + 1) * CHI]
                for r2 in range(D // 2):
                    o0 = out[2 * r2 * DP:(2 * r2 + 1) * DP]
                    o1 = out[(2 * r2 + 1) * DP:(2 * r2 + 2) * DP]
                    top = jnp.concatenate([o0[:, :HALF], o1[:, :HALF]], axis=1)
                    low = jnp.concatenate([o0[:, HALF:], o1[:, HALF:]], axis=1)
                    ys[r2, 4 * q + i] = jnp.concatenate([top, low], axis=0).astype(BF)
        run(16 // 4, body)

    def step_three(g, ys, k):
        def body(n2):
            lhs = jnp.concatenate([ys[i, pl.ds(8 * k, 8)].reshape(384, CHI) for i in range(10)], axis=1)
            rhs = jnp.concatenate([pair_half(g, i) for i in range(10)], axis=1)
            acc[k] = dot(lhs, rhs, NT)
        body(0)
        pad[0] = acc[k, :, :HALF]
        pad[1] = acc[k, :, HALF:]

    def sum_a(slot, part):
        sq_s[slot, 0] = part
        return [send(sq_s.at[slot, 0], sq_r.at[slot, i], p) for i, p in enumerate((SIB, YP, SY))]

    def sum_b(slot, cps, dcol):
        recv(cps)
        sq_s[slot, 1] = sq_s[slot, 0] + sq_r[slot, 0] + sq_r[slot, 1] + sq_r[slot, 2]
        return [
            send(sq_s.at[slot, 1], sq_r.at[slot, 3 + d], at(dcol, 0, d))
            for d in range(4) if d > 0 or dcol != 0
        ]

    def sum_c(slot, cps):
        recv(cps)
        first = sq_r[slot, 3] if len(cps) == 4 else sq_s[slot, 1]
        total = jnp.sum(first + sq_r[slot, 4] + sq_r[slot, 5] + sq_r[slot, 6])
        return jnp.sqrt(float(CHI * D * CHI) / total)

    def squares(v):
        s = v * v
        if s.shape[1] > HALF:
            s = s[:, :HALF] + s[:, HALF:]
        return s[:8] + s[8:]

    recv([p_al_y, lb_y])
    lb[1] = pad_own(lbp).astype(BF)
    alt[:, 384:] = pad_partner(g_al, p_al).T.astype(BF)
    al_sib = to_sib(g_al, al_x)
    hand_up(r_x, g_r)
    recv(al_sib)
    ar_x = own_x(g_ar)
    step_one(lb, g_al)
    hand_down(r_x, g_r)
    rest_x(ar_x, g_ar, ar_y)
    step_two(w2, ys)
    hand_up(ar_x, g_ar)
    r_sib = to_sib(g_r, r_x)
    sib = []
    for ch in range(2):
        rhs = jnp.concatenate([ys[ch * 5 + i].reshape(768, CHI) for i in range(5)], axis=1)
        out = dot(alt[...], rhs)
        for i in range(5):
            r2 = ch * 5 + i
            zf[...] = out[:, i * CHI:(i + 1) * CHI].reshape(8, 2, ROWS, CHI)
            sib_s[r2] = zf[:, 1 - c].astype(BF)
            zk[r2] = zf[:, c]
        part_of = pl.ds(ch * 5, 5)
        sib.append(send(sib_s.at[part_of], sib_r.at[part_of], SIB))

    recv(p_ar_y)
    arj[1] = pad_partner(g_ar, p_ar).astype(BF)
    hand_down(ar_x, g_ar)
    rs = []
    for ch in range(2):
        recv(sib[ch])
        for k in range(5):
            r2 = ch * 5 + k
            v = zk[r2] + sib_r[r2].astype(F32)
            zk[r2] = v
            for yy in range(2):
                for xx in range(4):
                    x_s[xx, r2, yy] = v[yy * 4 + xx].astype(BF)
        part_of = pl.ds(ch * 5, 5)
        for d in (1, 2, 3):
            to = (x + d) % 4
            rs.append(send(x_s.at[to, part_of], x_r.at[d - 1, part_of], XP[d - 1]))
    recv(r_sib)
    step_one(arj, g_r)
    step_two(w4, ys2)
    ar_sib = to_sib(g_ar, ar_x)
    ac_x = straight_both(g_ac, ac_y)

    def right_block(yy):
        k = (y + yy) % 2
        step_three(g_ar, ys2, k)
        for h in range(2):
            for l in range(D):
                rs_s[h, yy, l] = row(h, l).astype(BF)
        return [
            send(rs_s.at[y, yy], n_in.at[y, yy], at(-1)),
            send(rs_s.at[1 - y, yy], n_in.at[y, yy], at(-1, 1)),
        ]

    recv(ar_sib)
    n_col = [right_block(0), right_block(1)]
    recv(rs)
    part = jnp.zeros((8, HALF), F32)
    for r2 in range(D // 2):
        for yy in range(2):
            v = zk[r2, yy * 4 + x]
            for d in range(3):
                v = v + x_r[d, r2, yy].astype(F32)
            lp[r2, yy] = v.astype(BF)
            part = part + squares(v)
    l_col = [send(lp, lr.at[y], at(1)), send(lp, lr.at[y], at(1, 1))]
    left_sum = sum_b(1, sum_a(1, part), 1)

    part = jnp.zeros((8, HALF), F32)
    n_x = []
    for yy in range(2):
        recv(n_col[yy])
        for l in range(D):
            v = n_in[0, yy, l].astype(F32) + n_in[1, yy, l].astype(F32)
            n_sum[yy, l] = v
            g_n[c, x, yy, l] = v.astype(BF)
            part = part + squares(v)
        n_x += straight(g_n.at[c, x, yy])
    n_snd[...] = n_sum[1 - y].astype(BF)
    n_y = send(n_snd, n_oth, YP)
    right_sum = sum_a(0, part)
    ac_sib = all_to_sib(g_ac, ac_x)
    recv(l_col)
    for l in range(D):
        h = l % 2
        for src in range(2):
            for yy in range(2):
                v = lr[src, l // 2, yy, :, h * HALF:(h + 1) * HALF].astype(F32)
                ln[yy, src, pl.ds(l, ROWS, stride=DP), :] = v
    for yy in range(2):
        lb[yy] = jnp.concatenate([ln[yy, 0], ln[yy, 1]], axis=1).astype(BF)
    right_sum = sum_b(0, right_sum, 0)
    recv(ac_sib)
    step_one(lb, g_ac)
    scale = sum_c(1, left_sum)
    step_two(w2, ys, scale)
    n_sib = all_to_sib(g_n, n_x)
    for l in range(D):
        for src in range(2):
            v = ln[y, src, pl.ds(l, ROWS, stride=DP), :] * scale
            new_left_ref[l, :, src * HALF:(src + 1) * HALF] = v
    recv(n_sib)
    step_three(g_n, ys, 1 - y)
    cy_s[...] = acc[1 - y].astype(BF)
    cy = send(cy_s, cy_r, YP)
    step_three(g_n, ys, y)
    scale = sum_c(0, right_sum)
    recv(n_y)
    for l in range(D):
        a, b = n_sum[y, l] * scale, n_oth[l].astype(F32) * scale
        new_right_ref[l, :, :HALF] = jnp.where(y == 0, a, b)
        new_right_ref[l, :, HALF:] = jnp.where(y == 0, b, a)
    recv(cy)
    pad[0] = (acc[y, :, :HALF] + cy_r[:, :HALF].astype(F32)) * scale
    pad[1] = (acc[y, :, HALF:] + cy_r[:, HALF:].astype(F32)) * scale
    for n in range(D):
        new_center_ref[n, :, :HALF] = row(0, n)
        new_center_ref[n, :, HALF:] = row(1, n)
    for cp in started:
        cp.wait_send()


def on_device(left_iso, right_iso, center, site_tensor, left_env, right_env):
    out = jax.ShapeDtypeStruct((D, ROWS, CHI), F32)
    vm = pl.BlockSpec(memory_space=pltpu.VMEM)
    V = pltpu.VMEM
    res = pl.pallas_call(
        kernel,
        out_shape=[out] * 3,
        in_specs=[vm] * 6,
        out_specs=[vm] * 3,
        scratch_shapes=[
            V((2, ROWS * DP, HALF), F32),
            *[V((D, ROWS, HALF), BF)] * 3,
            *[V((D, ROWS, CHI), BF)] * 2,
            *[V((2, 4, 2, D, ROWS, HALF), BF)] * 5,
            *[V((2, ROWS * DP, CHI), BF)] * 2,
            V((CHI, 2 * ROWS * DP), BF),
            V((D * DP, D * DP), BF), V((D * DP, D * DP), BF),
            V((D // 2, 32, DP, CHI), F32),
            *[V((D // 2, 16, 2 * DP, CHI), BF)] * 2,
            V((2, ROWS * DP, CHI), F32),
            V((8, 2, ROWS, CHI), F32),
            V((D // 2, 8, ROWS, CHI), F32),
            V((D // 2, 8, ROWS, CHI), BF), V((D // 2, 8, ROWS, CHI), BF),
            V((4, D // 2, 2, ROWS, CHI), BF), V((3, D // 2, 2, ROWS, CHI), BF),
            V((8, HALF), F32),
            V((D // 2, 2, ROWS, CHI), BF), V((2, D // 2, 2, ROWS, CHI), BF),
            V((2, 2, ROWS * DP, HALF), F32),
            V((2, 2, D, ROWS, HALF), BF), V((2, 2, D, ROWS, HALF), BF),
            V((2, D, ROWS, HALF), F32),
            V((D, ROWS, HALF), BF), V((D, ROWS, HALF), BF),
            V((ROWS * DP, CHI), BF), V((ROWS * DP, CHI), BF),
            V((2, 2, 8, HALF), F32), V((2, 7, 8, HALF), F32),
            pltpu.SemaphoreType.DMA((80,)), pltpu.SemaphoreType.DMA((80,)),
        ],
        compiler_params=pltpu.CompilerParams(
            collective_id=0, has_side_effects=True, vmem_limit_bytes=56 * 2**20
        ),
        cost_estimate=pl.CostEstimate(flops=9 * 10**9, bytes_accessed=3 * 10**6, transcendentals=0),
        name="vumps",
    )(
        *(v[0].transpose(1, 0, 2) for v in (left_iso, right_iso, center)),
        site_tensor[0],
        *(v[0].transpose(1, 0, 2) for v in (left_env, right_env)),
    )
    return tuple(o.transpose(1, 0, 2)[None] for o in res)


def solution(mesh):
    spec = P("col", "chi", None, None)
    return jax.shard_map(
        on_device,
        mesh=mesh,
        in_specs=(spec, spec, spec, P("col", None, None), spec, spec),
        out_specs=(spec, spec, spec),
        check_vma=False,
    )
```

```python
import jax
import jax.numpy as jnp
from jax import lax
from jax.experimental import pallas as pl
from jax.experimental.pallas import tpu as pltpu
from jax.sharding import PartitionSpec as P

MESH = pl.DeviceIdType.MESH
BF = jnp.bfloat16
F32 = jnp.float32
D = 20
DP = 24
CHI = 256
ROWS = 16
HALF = 128
NT = (((1,), (1,)), ((), ()))
NN = (((1,), (0,)), ((), ()))


def dot(a, b, dims=NN):
    return lax.dot_general(a, b, dims, preferred_element_type=F32)


def kernel(
    al_ref, ar_ref, ac_ref, w_ref, l_ref, r_ref,
    new_left_ref, new_right_ref, new_center_ref,
    pad, half_r, p_al, p_ar, lbf, lbp,
    g_al, g_ar, g_ac, g_r, g_n,
    lb, arj, alt, w2, w4, xs, ys, ys2, acc, zf, zk,
    sib_s, sib_r, x_s, x_r, raw, lp, lr, ln,
    rs_s, n_in, n_sum, n_snd, n_oth, cy_s, cy_r, sq_s, sq_r, sc_s, sc_r,
    send_sem, recv_sem,
):
    col = lax.axis_index("col")
    me = lax.axis_index("chi")
    y, x, c = me // 8, (me // 2) % 4, me % 2
    cols = lax.axis_size("col")

    def at(dcol=0, dy=0, dx=0, dc=0):
        chi = ((y + dy) % 2) * 8 + ((x + dx) % 4) * 2 + (c + dc) % 2
        return ((col + dcol + cols) % cols, chi)

    SIB, YP = at(dc=1), at(dy=1)
    XP = [at(dx=d) for d in (1, 2, 3)]

    barrier = pltpu.get_barrier_semaphore()
    SY = at(dy=1, dc=1)
    peers = [SIB, YP, SY] + XP + [at(1), at(1, 1), at(-1), at(-1, 1)]
    for p in peers:
        pl.semaphore_signal(barrier, inc=1, device_id=p, device_id_type=MESH)

    count = [0]
    started = []

    def send(src, dst, target):
        i = count[0]
        count[0] += 1
        cp = pltpu.make_async_remote_copy(
            src_ref=src, dst_ref=dst, send_sem=send_sem.at[i], recv_sem=recv_sem.at[i],
            device_id=target, device_id_type=MESH,
        )
        cp.start()
        started.append(cp)
        return cp

    def recv(cps):
        for cp in cps if isinstance(cps, list) else [cps]:
            cp.wait_recv()

    def own_half(v):
        return jnp.where(y == 0, v[..., :HALF], v[..., HALF:])

    def other_half(v):
        return jnp.where(y == 0, v[..., HALF:], v[..., :HALF])

    def lanes(ref, h):
        return ref.at[:, :, pl.ds(pl.multiple_of(h * HALF, HALF), HALF)]

    def put(h, u, v):
        pad[h, pl.ds(u, ROWS, stride=DP), :] = v.astype(F32)

    def row(h, u):
        return pad[h, pl.ds(u, ROWS, stride=DP), :]

    def padded():
        return jnp.concatenate([pad[0], pad[1]], axis=1)

    def pad_own(ref):
        for u in range(D):
            v = ref[u].astype(F32)
            put(0, u, v[:, :HALF])
            put(1, u, v[:, HALF:])
        return padded()

    def pad_partner(g, p):
        for u in range(D):
            put(y, u, g[c, x, 1 - y, u])
            put(1 - y, u, p[u])
        return padded()

    def to_y(g, src):
        return send(src, g.at[c, x, y], YP)

    def both_ways(g, yy):
        ref = g.at[c, x, yy]
        return send(ref, ref, XP[0]), send(ref, ref, XP[2])

    def own_x(g):
        return list(both_ways(g, y))

    def rest_x(ring, g, first):
        recv(first)
        ring.extend(both_ways(g, 1 - y))

    def hand_up(ring, g):
        recv(ring[0])
        ref = g.at[c, (x + 3) % 4, y]
        ring.append(send(ref, ref, XP[0]))

    def hand_down(ring, g):
        recv(ring[3])
        ref = g.at[c, (x + 1) % 4, 1 - y]
        ring.append(send(ref, ref, XP[2]))

    def to_sib(g, ring):
        recv([ring[1], ring[2], ring[4], ring[5]])
        return send(g.at[c], g.at[c], SIB)

    def straight(ref):
        return [send(ref, ref, p) for p in XP]

    def straight_both(g, first):
        cps = straight(g.at[c, x, y])
        recv(first)
        return cps + straight(g.at[c, x, 1 - y])

    def all_to_sib(g, cps):
        recv(cps)
        return send(g.at[c], g.at[c], SIB)

    g_al[c, x, y] = own_half(al_ref[...])
    half_r[...] = other_half(r_ref[...]).astype(BF)
    g_r[c, x, y] = own_half(r_ref[...]).astype(BF)
    pad[...] = jnp.zeros_like(pad)
    pl.semaphore_wait(barrier, len(peers))
    al_y = to_y(g_al, lanes(al_ref, 1 - y))
    al_x = own_x(g_al)
    r_y = to_y(g_r, half_r)
    lbf[...] = l_ref[...].astype(BF)
    lb_y = send(lbf, lbp, YP)
    p_al_y = send(lanes(al_ref, y), p_al, YP)
    ar_y = to_y(g_ar, lanes(ar_ref, 1 - y))
    p_ar_y = send(lanes(ar_ref, y), p_ar, YP)
    ac_y = to_y(g_ac, lanes(ac_ref, 1 - y))
    rest_x(al_x, g_al, al_y)
    hand_up(al_x, g_al)
    r_x = own_x(g_r)
    g_ar[c, x, y] = own_half(ar_ref[...])
    g_ac[c, x, y] = own_half(ac_ref[...])
    lb[0] = pad_own(l_ref).astype(BF)
    alt[:, :384] = pad_own(al_ref).T.astype(BF)
    hand_down(al_x, g_al)
    rest_x(r_x, g_r, r_y)
    arj[0] = pad_own(ar_ref).astype(BF)
    ln[...] = jnp.zeros_like(ln)

    def spread(other):
        i = lax.broadcasted_iota(jnp.int32, (D * DP, D * D), 0)
        j = lax.broadcasted_iota(jnp.int32, (D * DP, D * D), 1)
        big = (i * 2731) >> 16
        small = i - big * DP
        want = small * D + big if other else big * D + small
        return jnp.where((small < D) & (j == want), 1.0, 0.0).astype(BF)

    t = dot(spread(True), w_ref[...]).astype(BF)
    w4[...] = dot(t, spread(False), NT).astype(BF)
    w2[...] = w4[...].astype(F32).T.astype(BF)

    def full_rows(g, u):
        return jnp.concatenate(
            [g[cc, xx, yy, u] for yy in range(2) for xx in range(4) for cc in range(2)], axis=0
        )

    def pair_half(g, u2):
        return jnp.concatenate([full_rows(g, 2 * u2), full_rows(g, 2 * u2 + 1)], axis=1)

    def run(n, body):
        lax.fori_loop(0, n, lambda k, _: body(k), None)

    def step_one(lhs_ref, g):
        def body(q):
            rhs = jnp.concatenate([pair_half(g, 5 * q + i) for i in range(5)], axis=1)
            for k in range(2):
                out = dot(lhs_ref[k], rhs)
                for i in range(5):
                    xs[5 * q + i, 16 * k:16 * k + 16] = out[:, i * CHI:(i + 1) * CHI].reshape(16, DP, CHI)
        run(D // 2 // 5, body)

    def step_two(m_ref, ys, scale=None):
        def body(q):
            cols_ = []
            for i in range(4):
                p = 4 * q + i
                rows = []
                for u2 in range(D // 2):
                    v0, v1 = xs[u2, 2 * p], xs[u2, 2 * p + 1]
                    rows.append(jnp.concatenate([v0[:, :HALF], v1[:, :HALF]], axis=1))
                    rows.append(jnp.concatenate([v0[:, HALF:], v1[:, HALF:]], axis=1))
                cols_.append(jnp.concatenate(rows, axis=0).astype(BF))
            both = dot(m_ref[...], jnp.concatenate(cols_, axis=1))
            if scale is not None:
                both = both * scale
            for i in range(4):
                out = both[:, i * CHI:(i + 1) * CHI]
                for r2 in range(D // 2):
                    o0 = out[2 * r2 * DP:(2 * r2 + 1) * DP]
                    o1 = out[(2 * r2 + 1) * DP:(2 * r2 + 2) * DP]
                    top = jnp.concatenate([o0[:, :HALF], o1[:, :HALF]], axis=1)
                    low = jnp.concatenate([o0[:, HALF:], o1[:, HALF:]], axis=1)
                    ys[r2, 4 * q + i] = jnp.concatenate([top, low], axis=0).astype(BF)
        run(16 // 4, body)

    def step_three(g, ys, k):
        def body(n2):
            lhs = jnp.concatenate([ys[i, pl.ds(8 * k, 8)].reshape(384, CHI) for i in range(10)], axis=1)
            rhs = jnp.concatenate([pair_half(g, i) for i in range(10)], axis=1)
            acc[k] = dot(lhs, rhs, NT)
        body(0)
        pad[0] = acc[k, :, :HALF]
        pad[1] = acc[k, :, HALF:]

    def sum_a(slot, part):
        sq_s[slot, 0] = part
        return [send(sq_s.at[slot, 0], sq_r.at[slot, i], p) for i, p in enumerate((SIB, YP, SY))]

    def sum_b(slot, cps):
        recv(cps)
        sq_s[slot, 1] = sq_s[slot, 0] + sq_r[slot, 0] + sq_r[slot, 1] + sq_r[slot, 2]
        return [send(sq_s.at[slot, 1], sq_r.at[slot, 3 + d], XP[d]) for d in range(3)]

    def sum_c(slot, cps):
        recv(cps)
        total = jnp.sum(sq_s[slot, 1] + sq_r[slot, 3] + sq_r[slot, 4] + sq_r[slot, 5])
        return jnp.sqrt(float(CHI * D * CHI) / total)

    def squares(v):
        s = v * v
        if s.shape[1] > HALF:
            s = s[:, :HALF] + s[:, HALF:]
        return s[:8] + s[8:]

    recv([p_al_y, lb_y])
    lb[1] = pad_own(lbp).astype(BF)
    alt[:, 384:] = pad_partner(g_al, p_al).T.astype(BF)
    al_sib = to_sib(g_al, al_x)
    hand_up(r_x, g_r)
    recv(al_sib)
    ar_x = own_x(g_ar)
    step_one(lb, g_al)
    hand_down(r_x, g_r)
    rest_x(ar_x, g_ar, ar_y)
    step_two(w2, ys)
    hand_up(ar_x, g_ar)
    r_sib = to_sib(g_r, r_x)
    sib = []
    for ch in range(2):
        rhs = jnp.concatenate([ys[ch * 5 + i].reshape(768, CHI) for i in range(5)], axis=1)
        out = dot(alt[...], rhs)
        for i in range(5):
            r2 = ch * 5 + i
            zf[...] = out[:, i * CHI:(i + 1) * CHI].reshape(8, 2, ROWS, CHI)
            sib_s[r2] = zf[:, 1 - c].astype(BF)
            zk[r2] = zf[:, c]
        part_of = pl.ds(ch * 5, 5)
        sib.append(send(sib_s.at[part_of], sib_r.at[part_of], SIB))

    recv(p_ar_y)
    arj[1] = pad_partner(g_ar, p_ar).astype(BF)
    hand_down(ar_x, g_ar)
    rs = []
    for ch in range(2):
        recv(sib[ch])
        for k in range(5):
            r2 = ch * 5 + k
            v = zk[r2] + sib_r[r2].astype(F32)
            zk[r2] = v
            for yy in range(2):
                for xx in range(4):
                    x_s[xx, r2, yy] = v[yy * 4 + xx].astype(BF)
        part_of = pl.ds(ch * 5, 5)
        for d in (1, 2, 3):
            to = (x + d) % 4
            rs.append(send(x_s.at[to, part_of], x_r.at[d - 1, part_of], XP[d - 1]))
    recv(r_sib)
    step_one(arj, g_r)
    ar_sib = to_sib(g_ar, ar_x)
    ac_x = straight_both(g_ac, ac_y)
    step_two(w4, ys2)

    def right_block(yy):
        k = (y + yy) % 2
        step_three(g_ar, ys2, k)
        for h in range(2):
            for l in range(D):
                rs_s[h, yy, l] = row(h, l).astype(BF)
        return [
            send(rs_s.at[y, yy], n_in.at[y, yy], at(-1)),
            send(rs_s.at[1 - y, yy], n_in.at[y, yy], at(-1, 1)),
        ]

    recv(ar_sib)
    n_col = [right_block(0), right_block(1)]
    recv(rs)
    part = jnp.zeros((8, HALF), F32)
    for r2 in range(D // 2):
        for yy in range(2):
            v = zk[r2, yy * 4 + x]
            for d in range(3):
                v = v + x_r[d, r2, yy].astype(F32)
            lp[r2, yy] = v.astype(BF)
            part = part + squares(v)
    l_col = [send(lp, lr.at[y], at(1)), send(lp, lr.at[y], at(1, 1))]
    left_sum = sum_b(1, sum_a(1, part))

    part = jnp.zeros((8, HALF), F32)
    n_x = []
    for yy in range(2):
        recv(n_col[yy])
        for l in range(D):
            v = n_in[0, yy, l].astype(F32) + n_in[1, yy, l].astype(F32)
            n_sum[yy, l] = v
            g_n[c, x, yy, l] = v.astype(BF)
            part = part + squares(v)
        n_x += straight(g_n.at[c, x, yy])
    n_snd[...] = n_sum[1 - y].astype(BF)
    n_y = send(n_snd, n_oth, YP)
    right_sum = sum_a(0, part)
    sc_s[...] = jnp.full((8, HALF), 1.0, F32) * sum_c(1, left_sum)
    l_sc = send(sc_s, sc_r, at(1))
    ac_sib = all_to_sib(g_ac, ac_x)
    recv(l_col)
    for l in range(D):
        h = l % 2
        for src in range(2):
            for yy in range(2):
                v = lr[src, l // 2, yy, :, h * HALF:(h + 1) * HALF].astype(F32)
                ln[yy, src, pl.ds(l, ROWS, stride=DP), :] = v
    for yy in range(2):
        lb[yy] = jnp.concatenate([ln[yy, 0], ln[yy, 1]], axis=1).astype(BF)
    right_sum = sum_b(0, right_sum)
    recv(ac_sib)
    step_one(lb, g_ac)
    recv(l_sc)
    scale = sc_r[0:1, 0:1]
    step_two(w2, ys, scale)
    n_sib = []
    for yy in range(2):
        recv(n_x[3 * yy:3 * yy + 3])
        ref = g_n.at[c, :, yy]
        n_sib.append(send(ref, ref, SIB))
    for l in range(D):
        for src in range(2):
            v = ln[y, src, pl.ds(l, ROWS, stride=DP), :] * scale
            new_left_ref[l, :, src * HALF:(src + 1) * HALF] = v.astype(BF)
    recv(n_sib)
    step_three(g_n, ys, 1 - y)
    for n in range(D):
        cy_s[n] = jnp.concatenate([row(0, n), row(1, n)], axis=1).astype(BF)
    cy = send(cy_s, cy_r, YP)
    step_three(g_n, ys, y)
    scale = sum_c(0, right_sum)
    recv(n_y)
    for l in range(D):
        a, b = n_sum[y, l] * scale, n_oth[l].astype(F32) * scale
        new_right_ref[l, :, :HALF] = jnp.where(y == 0, a, b).astype(BF)
        new_right_ref[l, :, HALF:] = jnp.where(y == 0, b, a).astype(BF)
    recv(cy)
    for n in range(D):
        v = jnp.concatenate([row(0, n), row(1, n)], axis=1) + cy_r[n].astype(F32)
        new_center_ref[n] = (v * scale).astype(BF)
    for cp in started:
        cp.wait_send()


def on_device(left_iso, right_iso, center, site_tensor, left_env, right_env):
    out = jax.ShapeDtypeStruct((D, ROWS, CHI), BF)
    vm = pl.BlockSpec(memory_space=pltpu.VMEM)
    V = pltpu.VMEM
    res = pl.pallas_call(
        kernel,
        out_shape=[out] * 3,
        in_specs=[vm] * 6,
        out_specs=[vm] * 3,
        scratch_shapes=[
            V((2, ROWS * DP, HALF), F32),
            *[V((D, ROWS, HALF), BF)] * 3,
            *[V((D, ROWS, CHI), BF)] * 2,
            *[V((2, 4, 2, D, ROWS, HALF), BF)] * 5,
            *[V((2, ROWS * DP, CHI), BF)] * 2,
            V((CHI, 2 * ROWS * DP), BF),
            V((D * DP, D * DP), BF), V((D * DP, D * DP), BF),
            V((D // 2, 32, DP, CHI), F32),
            *[V((D // 2, 16, 2 * DP, CHI), BF)] * 2,
            V((2, ROWS * DP, CHI), F32),
            V((8, 2, ROWS, CHI), F32),
            V((D // 2, 8, ROWS, CHI), F32),
            V((D // 2, 8, ROWS, CHI), BF), V((D // 2, 8, ROWS, CHI), BF),
            V((4, D // 2, 2, ROWS, CHI), BF), V((3, D // 2, 2, ROWS, CHI), BF),
            V((8, HALF), F32),
            V((D // 2, 2, ROWS, CHI), BF), V((2, D // 2, 2, ROWS, CHI), BF),
            V((2, 2, ROWS * DP, HALF), F32),
            V((2, 2, D, ROWS, HALF), BF), V((2, 2, D, ROWS, HALF), BF),
            V((2, D, ROWS, HALF), F32),
            V((D, ROWS, HALF), BF), V((D, ROWS, HALF), BF),
            V((D, ROWS, CHI), BF), V((D, ROWS, CHI), BF),
            V((2, 2, 8, HALF), F32), V((2, 6, 8, HALF), F32),
            V((8, HALF), F32), V((8, HALF), F32),
            pltpu.SemaphoreType.DMA((80,)), pltpu.SemaphoreType.DMA((80,)),
        ],
        compiler_params=pltpu.CompilerParams(
            collective_id=0, has_side_effects=True, vmem_limit_bytes=56 * 2**20
        ),
        cost_estimate=pl.CostEstimate(flops=9 * 10**9, bytes_accessed=3 * 10**6, transcendentals=0),
        name="vumps",
    )(
        *(v[0].transpose(1, 0, 2) for v in (left_iso, right_iso, center)),
        site_tensor[0],
        *(v[0].transpose(1, 0, 2) for v in (left_env, right_env)),
    )
    return tuple(o.astype(F32).transpose(1, 0, 2)[None] for o in res)


def solution(mesh):
    spec = P("col", "chi", None, None)
    return jax.shard_map(
        on_device,
        mesh=mesh,
        in_specs=(spec, spec, spec, P("col", None, None), spec, spec),
        out_specs=(spec, spec, spec),
        check_vma=False,
    )
```

```python
import jax
import jax.numpy as jnp
from jax import lax
from jax.experimental import pallas as pl
from jax.experimental.pallas import tpu as pltpu
from jax.sharding import PartitionSpec as P

MESH = pl.DeviceIdType.MESH
BF = jnp.bfloat16
F32 = jnp.float32
D = 20
DP = 24
CHI = 256
ROWS = 16
HALF = 128
NT = (((1,), (1,)), ((), ()))
NN = (((1,), (0,)), ((), ()))


def dot(a, b, dims=NN):
    return lax.dot_general(a, b, dims, preferred_element_type=F32)


def kernel(
    al_ref, ar_ref, ac_ref, w_ref, l_ref, r_ref,
    new_left_ref, new_right_ref, new_center_ref,
    pad, half_r, p_al, p_ar, lbf, lbp,
    g_al, g_ar, g_ac, g_r, g_n,
    lb, arj, alt, w2, w4, xs, ys, ys2, acc, zf, zk,
    sib_s, sib_r, x_s, x_r, raw, lp, lr, ln,
    rs_s, n_in, n_sum, n_snd, n_oth, cy_s, cy_r, sq_s, sq_r, sc_s, sc_r,
    send_sem, recv_sem,
):
    col = lax.axis_index("col")
    me = lax.axis_index("chi")
    y, x, c = me // 8, (me // 2) % 4, me % 2
    cols = lax.axis_size("col")

    def at(dcol=0, dy=0, dx=0, dc=0):
        chi = ((y + dy) % 2) * 8 + ((x + dx) % 4) * 2 + (c + dc) % 2
        return ((col + dcol + cols) % cols, chi)

    SIB, YP = at(dc=1), at(dy=1)
    XP = [at(dx=d) for d in (1, 2, 3)]

    barrier = pltpu.get_barrier_semaphore()
    SY = at(dy=1, dc=1)
    peers = [SIB, YP, SY] + XP + [at(1), at(1, 1), at(-1), at(-1, 1)]
    for p in peers:
        pl.semaphore_signal(barrier, inc=1, device_id=p, device_id_type=MESH)

    count = [0]
    started = []

    def send(src, dst, target):
        i = count[0]
        count[0] += 1
        cp = pltpu.make_async_remote_copy(
            src_ref=src, dst_ref=dst, send_sem=send_sem.at[i], recv_sem=recv_sem.at[i],
            device_id=target, device_id_type=MESH,
        )
        cp.start()
        started.append(cp)
        return cp

    def recv(cps):
        for cp in cps if isinstance(cps, list) else [cps]:
            cp.wait_recv()

    def own_half(v):
        return jnp.where(y == 0, v[..., :HALF], v[..., HALF:])

    def other_half(v):
        return jnp.where(y == 0, v[..., HALF:], v[..., :HALF])

    def lanes(ref, h):
        return ref.at[:, :, pl.ds(pl.multiple_of(h * HALF, HALF), HALF)]

    def put(h, u, v):
        pad[h, pl.ds(u, ROWS, stride=DP), :] = v.astype(F32)

    def row(h, u):
        return pad[h, pl.ds(u, ROWS, stride=DP), :]

    def padded():
        return jnp.concatenate([pad[0], pad[1]], axis=1)

    def pad_own(ref):
        for u in range(D):
            v = ref[u].astype(F32)
            put(0, u, v[:, :HALF])
            put(1, u, v[:, HALF:])
        return padded()

    def pad_partner(g, p):
        for u in range(D):
            put(y, u, g[c, x, 1 - y, u])
            put(1 - y, u, p[u])
        return padded()

    def to_y(g, src):
        return send(src, g.at[c, x, y], YP)

    def both_ways(g, yy):
        ref = g.at[c, x, yy]
        return send(ref, ref, XP[0]), send(ref, ref, XP[2])

    def own_x(g):
        return list(both_ways(g, y))

    def rest_x(ring, g, first):
        recv(first)
        ring.extend(both_ways(g, 1 - y))

    def hand_up(ring, g):
        recv(ring[0])
        ref = g.at[c, (x + 3) % 4, y]
        ring.append(send(ref, ref, XP[0]))

    def hand_down(ring, g):
        recv(ring[3])
        ref = g.at[c, (x + 1) % 4, 1 - y]
        ring.append(send(ref, ref, XP[2]))

    def to_sib(g, ring):
        recv([ring[1], ring[2], ring[4], ring[5]])
        return send(g.at[c], g.at[c], SIB)

    def straight(ref):
        return [send(ref, ref, p) for p in XP]

    def straight_both(g, first):
        cps = straight(g.at[c, x, y])
        recv(first)
        return cps + straight(g.at[c, x, 1 - y])

    def all_to_sib(g, cps):
        recv(cps)
        return send(g.at[c], g.at[c], SIB)

    g_al[c, x, y] = own_half(al_ref[...])
    half_r[...] = other_half(r_ref[...]).astype(BF)
    g_r[c, x, y] = own_half(r_ref[...]).astype(BF)
    pad[...] = jnp.zeros_like(pad)
    pl.semaphore_wait(barrier, len(peers))
    al_y = to_y(g_al, lanes(al_ref, 1 - y))
    al_x = own_x(g_al)
    r_y = to_y(g_r, half_r)
    lbf[...] = l_ref[...].astype(BF)
    lb_y = send(lbf, lbp, YP)
    p_al_y = send(lanes(al_ref, y), p_al, YP)
    ar_y = to_y(g_ar, lanes(ar_ref, 1 - y))
    p_ar_y = send(lanes(ar_ref, y), p_ar, YP)
    ac_y = to_y(g_ac, lanes(ac_ref, 1 - y))
    rest_x(al_x, g_al, al_y)
    hand_up(al_x, g_al)
    r_x = own_x(g_r)
    g_ar[c, x, y] = own_half(ar_ref[...])
    g_ac[c, x, y] = own_half(ac_ref[...])
    lb[0] = pad_own(l_ref).astype(BF)
    alt[:, :384] = pad_own(al_ref).T.astype(BF)
    hand_down(al_x, g_al)
    rest_x(r_x, g_r, r_y)
    arj[0] = pad_own(ar_ref).astype(BF)
    ln[...] = jnp.zeros_like(ln)

    def spread(other):
        i = lax.broadcasted_iota(jnp.int32, (D * DP, D * D), 0)
        j = lax.broadcasted_iota(jnp.int32, (D * DP, D * D), 1)
        big = (i * 2731) >> 16
        small = i - big * DP
        want = small * D + big if other else big * D + small
        return jnp.where((small < D) & (j == want), 1.0, 0.0).astype(BF)

    t = dot(spread(True), w_ref[...]).astype(BF)
    w4[...] = dot(t, spread(False), NT).astype(BF)
    w2[...] = w4[...].astype(F32).T.astype(BF)

    def full_rows(g, u):
        return jnp.concatenate(
            [g[cc, xx, yy, u] for yy in range(2) for xx in range(4) for cc in range(2)], axis=0
        )

    def pair_half(g, u2):
        return jnp.concatenate([full_rows(g, 2 * u2), full_rows(g, 2 * u2 + 1)], axis=1)

    def run(n, body):
        lax.fori_loop(0, n, lambda k, _: body(k), None)

    def step_one(lhs_ref, g):
        def body(q):
            rhs = jnp.concatenate([pair_half(g, 5 * q + i) for i in range(5)], axis=1)
            for k in range(2):
                out = dot(lhs_ref[k], rhs)
                for i in range(5):
                    xs[5 * q + i, 16 * k:16 * k + 16] = out[:, i * CHI:(i + 1) * CHI].reshape(16, DP, CHI)
        run(D // 2 // 5, body)

    def step_two(m_ref, ys, scale=None):
        def body(q):
            cols_ = []
            for i in range(8):
                p = 8 * q + i
                rows = []
                for u2 in range(D // 2):
                    v0, v1 = xs[u2, 2 * p], xs[u2, 2 * p + 1]
                    rows.append(jnp.concatenate([v0[:, :HALF], v1[:, :HALF]], axis=1))
                    rows.append(jnp.concatenate([v0[:, HALF:], v1[:, HALF:]], axis=1))
                cols_.append(jnp.concatenate(rows, axis=0).astype(BF))
            both = dot(m_ref[...], jnp.concatenate(cols_, axis=1))
            if scale is not None:
                both = both * scale
            for i in range(8):
                out = both[:, i * CHI:(i + 1) * CHI]
                for r2 in range(D // 2):
                    o0 = out[2 * r2 * DP:(2 * r2 + 1) * DP]
                    o1 = out[(2 * r2 + 1) * DP:(2 * r2 + 2) * DP]
                    top = jnp.concatenate([o0[:, :HALF], o1[:, :HALF]], axis=1)
                    low = jnp.concatenate([o0[:, HALF:], o1[:, HALF:]], axis=1)
                    ys[r2, 8 * q + i] = jnp.concatenate([top, low], axis=0).astype(BF)
        run(16 // 8, body)

    def step_three(g, ys, k):
        def body(n2):
            lhs = jnp.concatenate([ys[i, pl.ds(8 * k, 8)].reshape(384, CHI) for i in range(10)], axis=1)
            rhs = jnp.concatenate([pair_half(g, i) for i in range(10)], axis=1)
            acc[k] = dot(lhs, rhs, NT)
        body(0)
        pad[0] = acc[k, :, :HALF]
        pad[1] = acc[k, :, HALF:]

    def sum_a(slot, part):
        sq_s[slot, 0] = part
        return [send(sq_s.at[slot, 0], sq_r.at[slot, i], p) for i, p in enumerate((SIB, YP, SY))]

    def sum_b(slot, cps):
        recv(cps)
        sq_s[slot, 1] = sq_s[slot, 0] + sq_r[slot, 0] + sq_r[slot, 1] + sq_r[slot, 2]
        return [send(sq_s.at[slot, 1], sq_r.at[slot, 3 + d], XP[d]) for d in range(3)]

    def sum_c(slot, cps):
        recv(cps)
        total = jnp.sum(sq_s[slot, 1] + sq_r[slot, 3] + sq_r[slot, 4] + sq_r[slot, 5])
        return jnp.sqrt(float(CHI * D * CHI) / total)

    def squares(v):
        s = v * v
        if s.shape[1] > HALF:
            s = s[:, :HALF] + s[:, HALF:]
        return s[:8] + s[8:]

    recv([p_al_y, lb_y])
    lb[1] = pad_own(lbp).astype(BF)
    alt[:, 384:] = pad_partner(g_al, p_al).T.astype(BF)
    al_sib = to_sib(g_al, al_x)
    hand_up(r_x, g_r)
    recv(al_sib)
    ar_x = own_x(g_ar)
    step_one(lb, g_al)
    hand_down(r_x, g_r)
    rest_x(ar_x, g_ar, ar_y)
    step_two(w2, ys)
    hand_up(ar_x, g_ar)
    r_sib = to_sib(g_r, r_x)
    sib = []
    for ch in range(2):
        rhs = jnp.concatenate([ys[ch * 5 + i].reshape(768, CHI) for i in range(5)], axis=1)
        out = dot(alt[...], rhs)
        for i in range(5):
            r2 = ch * 5 + i
            zf[...] = out[:, i * CHI:(i + 1) * CHI].reshape(8, 2, ROWS, CHI)
            sib_s[r2] = zf[:, 1 - c].astype(BF)
            zk[r2] = zf[:, c]
        part_of = pl.ds(ch * 5, 5)
        sib.append(send(sib_s.at[part_of], sib_r.at[part_of], SIB))

    recv(p_ar_y)
    arj[1] = pad_partner(g_ar, p_ar).astype(BF)
    hand_down(ar_x, g_ar)
    rs = []
    for ch in range(2):
        recv(sib[ch])
        for k in range(5):
            r2 = ch * 5 + k
            v = zk[r2] + sib_r[r2].astype(F32)
            zk[r2] = v
            for yy in range(2):
                for xx in range(4):
                    x_s[xx, r2, yy] = v[yy * 4 + xx].astype(BF)
        part_of = pl.ds(ch * 5, 5)
        for d in (1, 2, 3):
            to = (x + d) % 4
            rs.append(send(x_s.at[to, part_of], x_r.at[d - 1, part_of], XP[d - 1]))
    recv(r_sib)
    step_one(arj, g_r)
    ar_sib = to_sib(g_ar, ar_x)
    ac_x = straight_both(g_ac, ac_y)
    step_two(w4, ys2)

    def right_block(yy):
        k = (y + yy) % 2
        step_three(g_ar, ys2, k)
        for h in range(2):
            for l in range(D):
                rs_s[h, yy, l] = row(h, l).astype(BF)
        return [
            send(rs_s.at[y, yy], n_in.at[y, yy], at(-1)),
            send(rs_s.at[1 - y, yy], n_in.at[y, yy], at(-1, 1)),
        ]

    recv(ar_sib)
    n_col = [right_block(0), right_block(1)]
    recv(rs)
    part = jnp.zeros((8, HALF), F32)
    for r2 in range(D // 2):
        for yy in range(2):
            v = zk[r2, yy * 4 + x]
            for d in range(3):
                v = v + x_r[d, r2, yy].astype(F32)
            lp[r2, yy] = v.astype(BF)
            part = part + squares(v)
    l_col = [send(lp, lr.at[y], at(1)), send(lp, lr.at[y], at(1, 1))]
    left_sum = sum_b(1, sum_a(1, part))

    part = jnp.zeros((8, HALF), F32)
    n_x = []
    for yy in range(2):
        recv(n_col[yy])
        for l in range(D):
            v = n_in[0, yy, l].astype(F32) + n_in[1, yy, l].astype(F32)
            n_sum[yy, l] = v
            g_n[c, x, yy, l] = v.astype(BF)
            part = part + squares(v)
        n_x += straight(g_n.at[c, x, yy])
    n_snd[...] = n_sum[1 - y].astype(BF)
    n_y = send(n_snd, n_oth, YP)
    right_sum = sum_a(0, part)
    sc_s[...] = jnp.full((8, HALF), 1.0, F32) * sum_c(1, left_sum)
    l_sc = send(sc_s, sc_r, at(1))
    ac_sib = all_to_sib(g_ac, ac_x)
    recv(l_col)
    for l in range(D):
        h = l % 2
        for src in range(2):
            for yy in range(2):
                v = lr[src, l // 2, yy, :, h * HALF:(h + 1) * HALF].astype(F32)
                ln[yy, src, pl.ds(l, ROWS, stride=DP), :] = v
    for yy in range(2):
        lb[yy] = jnp.concatenate([ln[yy, 0], ln[yy, 1]], axis=1).astype(BF)
    right_sum = sum_b(0, right_sum)
    recv(ac_sib)
    step_one(lb, g_ac)
    recv(l_sc)
    scale = sc_r[0:1, 0:1]
    step_two(w2, ys, scale)
    n_sib = []
    for yy in range(2):
        recv(n_x[3 * yy:3 * yy + 3])
        ref = g_n.at[c, :, yy]
        n_sib.append(send(ref, ref, SIB))
    for l in range(D):
        for src in range(2):
            v = ln[y, src, pl.ds(l, ROWS, stride=DP), :] * scale
            new_left_ref[l, :, src * HALF:(src + 1) * HALF] = v.astype(BF)
    recv(n_sib)
    step_three(g_n, ys, 1 - y)
    for n in range(D):
        cy_s[n] = jnp.concatenate([row(0, n), row(1, n)], axis=1).astype(BF)
    cy = send(cy_s, cy_r, YP)
    step_three(g_n, ys, y)
    scale = sum_c(0, right_sum)
    recv(n_y)
    for l in range(D):
        a, b = n_sum[y, l] * scale, n_oth[l].astype(F32) * scale
        new_right_ref[l, :, :HALF] = jnp.where(y == 0, a, b).astype(BF)
        new_right_ref[l, :, HALF:] = jnp.where(y == 0, b, a).astype(BF)
    recv(cy)
    for n in range(D):
        v = jnp.concatenate([row(0, n), row(1, n)], axis=1) + cy_r[n].astype(F32)
        new_center_ref[n] = (v * scale).astype(BF)
    for cp in started:
        cp.wait_send()


def on_device(left_iso, right_iso, center, site_tensor, left_env, right_env):
    out = jax.ShapeDtypeStruct((D, ROWS, CHI), BF)
    vm = pl.BlockSpec(memory_space=pltpu.VMEM)
    V = pltpu.VMEM
    res = pl.pallas_call(
        kernel,
        out_shape=[out] * 3,
        in_specs=[vm] * 6,
        out_specs=[vm] * 3,
        scratch_shapes=[
            V((2, ROWS * DP, HALF), F32),
            *[V((D, ROWS, HALF), BF)] * 3,
            *[V((D, ROWS, CHI), BF)] * 2,
            *[V((2, 4, 2, D, ROWS, HALF), BF)] * 5,
            *[V((2, ROWS * DP, CHI), BF)] * 2,
            V((CHI, 2 * ROWS * DP), BF),
            V((D * DP, D * DP), BF), V((D * DP, D * DP), BF),
            V((D // 2, 32, DP, CHI), F32),
            *[V((D // 2, 16, 2 * DP, CHI), BF)] * 2,
            V((2, ROWS * DP, CHI), F32),
            V((8, 2, ROWS, CHI), F32),
            V((D // 2, 8, ROWS, CHI), F32),
            V((D // 2, 8, ROWS, CHI), BF), V((D // 2, 8, ROWS, CHI), BF),
            V((4, D // 2, 2, ROWS, CHI), BF), V((3, D // 2, 2, ROWS, CHI), BF),
            V((8, HALF), F32),
            V((D // 2, 2, ROWS, CHI), BF), V((2, D // 2, 2, ROWS, CHI), BF),
            V((2, 2, ROWS * DP, HALF), F32),
            V((2, 2, D, ROWS, HALF), BF), V((2, 2, D, ROWS, HALF), BF),
            V((2, D, ROWS, HALF), F32),
            V((D, ROWS, HALF), BF), V((D, ROWS, HALF), BF),
            V((D, ROWS, CHI), BF), V((D, ROWS, CHI), BF),
            V((2, 2, 8, HALF), F32), V((2, 6, 8, HALF), F32),
            V((8, HALF), F32), V((8, HALF), F32),
            pltpu.SemaphoreType.DMA((80,)), pltpu.SemaphoreType.DMA((80,)),
        ],
        compiler_params=pltpu.CompilerParams(
            collective_id=0, has_side_effects=True, vmem_limit_bytes=56 * 2**20
        ),
        cost_estimate=pl.CostEstimate(flops=9 * 10**9, bytes_accessed=3 * 10**6, transcendentals=0),
        name="vumps",
    )(
        *(v[0].transpose(1, 0, 2) for v in (left_iso, right_iso, center)),
        site_tensor[0],
        *(v[0].transpose(1, 0, 2) for v in (left_env, right_env)),
    )
    return tuple(o.astype(F32).transpose(1, 0, 2)[None] for o in res)


def solution(mesh):
    spec = P("col", "chi", None, None)
    return jax.shard_map(
        on_device,
        mesh=mesh,
        in_specs=(spec, spec, spec, P("col", None, None), spec, spec),
        out_specs=(spec, spec, spec),
        check_vma=False,
    )
```
